32 devices in a mesh: tm: 4 (over y, x), space: 8 (over z, core).
Axes of the slice: x: 2, y: 2, z: 4, core: 2. Of those that a mesh axis runs over, the one named last changes fastest.
Arguments:
- activations: bfloat16 [32, 16, 8, 1024], P('tm', 'space'), may hold values from -6 to 6
- in_proj: bfloat16 [1024, 2176], replicated, may hold values from -0.1875 to 0.1875
- step_proj: bfloat16 [1024, 16], replicated, may hold values from -0.1875 to 0.1875
- step_bias: float32 [16], replicated, may hold values from -2 to 0
- decay_rates: float32 [16], replicated, may hold values from 0.005 to 0.5
- conv_kernel: float32 [3, 3, 1152], replicated, may hold values from -2 to 2
- conv_bias: float32 [1152], replicated, may hold values from -3 to 3
- skip_gain: float32 [16], replicated, may hold values from 0.5 to 1.5
- norm_gain: float32 [1024], replicated, may hold values from 0.5 to 1.5
- out_proj: bfloat16 [1024, 1024], replicated, may hold values from -0.1875 to 0.1875
- out_cotangent: bfloat16 [32, 16, 8, 1024], P('tm', 'space'), may hold values from -6 to 6
Outputs:
- layer_out: bfloat16 [32, 16, 8, 1024], P('tm', 'space')
- grad_input: bfloat16 [32, 16, 8, 1024], P('tm', 'space')
- grad_in_proj: float32 [1024, 2176], P(('tm', 'space'))
- grad_step_proj: float32 [1024, 16], P(('tm', 'space'))
- grad_out_proj_t: float32 [1024, 1024], P(('tm', 'space'))
- grad_conv_kernel: float32 [3, 3, 1152], replicated
- grad_conv_bias: float32 [1152], replicated
- grad_step_bias: float32 [16], replicated
- grad_decay_rates: float32 [16], replicated
- grad_skip_gain: float32 [16], replicated
- grad_norm_gain: float32 [1024], replicated
The draws below stay inside these ranges and needn't reach their ends.
All inputs are finite; a program needn't handle non-finite values.
Results may differ from the reference program's by a relative error of at most 0.015.
The reference program's roundings to bfloat16 on the way (of `gate_z`, `mixed_in`, `step_sizes`, `activated`, `ssd_out`, `normed` and `d_projected`) count: a program that leaves them out, or rounds other values in their place, can miss the bound.
Values may be sent and summed in bfloat16 or wider, within the bound.
A program may use at most 192 MiB of HBM per device.

```python
import math
import jax
import jax.numpy as jnp
from jax import lax

D = 1024
HEADS = 16
COLS = 8
FR_DEV = 8
EI = 1024
XC = 1152
FRAMES = 32
ROWS = 16


def strengthened(drawn, rng, source, target, shards_of, factor):
    owner, partner = [(jnp.arange(drawn.shape[position]) // (drawn.shape[position] // shards_of)).reshape([-1 if axis == position else 1 for axis in range(drawn.ndim)]) for position in (source, target)]
    chosen = jax.random.permutation(rng, shards_of)[partner]
    strong = (owner == chosen) | (owner == (partner + shards_of // 2) % shards_of)
    return jnp.where(strong, factor * drawn, drawn)


def level_of(key, extent, cuts, least, largest):
    def one(position, blocks):
        heights = jax.random.uniform(jax.random.fold_in(jax.random.fold_in(key, 6), position), (blocks,), jnp.float32, least / len(cuts), largest / len(cuts))
        return jnp.repeat(jnp.exp(heights), extent[position] // blocks).reshape((-1,) + (1,) * (len(extent) - position - 1))

    level = one(*cuts[0])
    for cut in cuts[1:]:
        level = level * one(*cut)
    return level


def noise(key, dims, deviation, most, shards=(), held_as=jnp.bfloat16):
    values = deviation * jax.random.normal(key, dims, jnp.float32)
    if shards:
        values = values * level_of(key, dims, shards, -0.22, 0.18)
    return jnp.clip(values, -most, most).astype(held_as)


def noise_with(own_key, dims, deviation, most, split, heavy, held_as=jnp.bfloat16):
    entries = deviation * jax.random.normal(own_key, dims, jnp.float32)
    if split:
        entries = entries * level_of(own_key, dims, split, -0.22, 0.18)
    return jnp.clip(strengthened(entries, jax.random.fold_in(own_key, 3), *heavy), -most, most).astype(held_as)


def setup_inputs(seed: int = 0) -> dict:
    arg_keys = jax.random.split(jax.random.key(seed), 12)
    activations = noise_with(arg_keys[0], (FRAMES, ROWS, COLS, D), 1.0, 6.0, ((0, 4), (1, 8)), (0, 3, 4, 2.0))
    in_proj = noise(arg_keys[1], (D, EI + XC), D ** -0.5, 0.1875)
    step_proj = noise(arg_keys[2], (D, HEADS), D ** -0.5, 0.1875)
    step_bias = jnp.clip(jax.random.uniform(arg_keys[3], (HEADS,), jnp.float32, -2.0, 0.0), -2.0, 0.0)
    decay_rates = jnp.clip(jnp.exp(jax.random.uniform(arg_keys[4], (HEADS,), jnp.float32, math.log(0.005), math.log(0.5))), 0.005, 0.5)
    conv_kernel = noise(arg_keys[5], (3, 3, XC), 9 ** -0.5, 2.0, (), jnp.float32)
    conv_bias = noise(arg_keys[6], (XC,), 0.5, 3.0, (), jnp.float32)
    skip_gain = jnp.clip(jax.random.uniform(arg_keys[7], (HEADS,), jnp.float32, 0.5, 1.5), 0.5, 1.5)
    norm_gain = jnp.clip(1.0 + 0.1 * jax.random.normal(arg_keys[8], (EI,), jnp.float32), 0.5, 1.5)
    out_proj = noise(arg_keys[9], (EI, D), EI ** -0.5, 0.1875)
    out_cotangent = noise_with(arg_keys[10], (FRAMES, ROWS, COLS, D), 1.0, 6.0, ((0, 4), (1, 8)), (1, 3, 8, 2.0))
    return dict(activations=activations, in_proj=in_proj, step_proj=step_proj, step_bias=step_bias, decay_rates=decay_rates, conv_kernel=conv_kernel, conv_bias=conv_bias, skip_gain=skip_gain, norm_gain=norm_gain, out_proj=out_proj, out_cotangent=out_cotangent)


top_precision = lax.Precision.HIGHEST
norm_eps = 1e-05

def ssd_block(heads_in, b_proj, c_proj, step_in, rate_in, gain_in, state_in):
    decay_step = step_in * rate_in
    running = jnp.cumsum(decay_step, axis=0)
    places = jnp.arange(heads_in.shape[0])
    causal = (places[:, None] >= places[None, :])[:, :, None, None]
    spread = running[:, None] - running[None, :]
    weights = jnp.where(causal, jnp.exp(-jnp.where(causal, spread, 0.0)), 0.0) * step_in[None, :]
    inner_cb = jnp.einsum('tkn,skn->tsk', c_proj, b_proj, precision=top_precision)
    intra_part = jnp.einsum('tskh,skhp->tkhp', weights * inner_cb[..., None], heads_in, precision=top_precision)
    carried = jnp.exp(-running)[..., None] * jnp.einsum('tkn,khpn->tkhp', c_proj, state_in, precision=top_precision)
    result = intra_part + carried + gain_in[:, None] * heads_in
    final_sum = running[-1]
    tail_weight = jnp.exp(running - final_sum[None]) * step_in
    state_out = jnp.exp(-final_sum)[..., None, None] * state_in + jnp.einsum('skh,skhp,skn->khpn', tail_weight, heads_in, b_proj, precision=top_precision)
    return (result, state_out)

def ssd_sequence(heads_in, b_proj, c_proj, step_in, rate_in, gain_in, block_len):
    block_count = heads_in.shape[0] // block_len

    def fold_blocks(array_in):
        return array_in.reshape((block_count, block_len) + array_in.shape[1:])
    start_state = jnp.zeros(heads_in.shape[1:4] + (b_proj.shape[2],), jnp.float32)

    def advance(carry_state, pieces):
        result, carry_state = ssd_block(pieces[0], pieces[1], pieces[2], pieces[3], rate_in, gain_in, carry_state)
        return (carry_state, result)
    final_state, results = lax.scan(advance, start_state, (fold_blocks(heads_in), fold_blocks(b_proj), fold_blocks(c_proj), fold_blocks(step_in)))
    return (results.reshape(heads_in.shape), final_state)

def gate_norm(ssd_float, gate_float, norm_gain):
    gated = ssd_float * jax.nn.silu(gate_float)
    scale_row = lax.rsqrt(lax.optimization_barrier(jnp.mean(gated * gated, axis=-1, keepdims=True)) + norm_eps)
    return gated * scale_row * norm_gain

def silu_slope(before):
    squashed = jax.nn.sigmoid(before)
    return squashed * (1.0 + before * (1.0 - squashed))

def conv_apply(padded, conv_kernel, conv_bias, row_count, col_count):
    accum = conv_kernel[0, 0] * padded[:, 0:row_count, 0:col_count]
    for row_off in range(3):
        for col_off in range(3):
            if row_off + col_off > 0:
                accum = accum + conv_kernel[row_off, col_off] * padded[:, row_off:row_off + row_count, col_off:col_off + col_count]
    return accum + conv_bias

def conv_transpose(d_padded, conv_kernel, row_count, col_count):
    accum = conv_kernel[0, 0] * d_padded[:, 2:2 + row_count, 2:2 + col_count]
    for row_off in range(3):
        for col_off in range(3):
            if row_off + col_off > 0:
                accum = accum + conv_kernel[row_off, col_off] * d_padded[:, 2 - row_off:2 - row_off + row_count, 2 - col_off:2 - col_off + col_count]
    return accum

def kernel_grad(d_before, padded, row_count, col_count):
    parts = []
    for row_off in range(3):
        for col_off in range(3):
            parts.append(lax.optimization_barrier(jnp.sum(d_before * padded[:, row_off:row_off + row_count, col_off:col_off + col_count], axis=(0, 1, 2))))
    return jnp.stack(parts).reshape(3, 3, -1)

def reference(activations, in_proj, step_proj, step_bias, decay_rates, conv_kernel, conv_bias, skip_gain, norm_gain, out_proj, out_cotangent):
    frame_count, row_count, col_count, model_width = activations.shape
    inner_w = out_proj.shape[0]
    head_count = step_proj.shape[1]
    head_dim = inner_w // head_count
    state_n = (in_proj.shape[1] - 2 * inner_w) // 2
    flat_act = activations.reshape(-1, model_width)
    projected = jnp.dot(flat_act, in_proj, preferred_element_type=jnp.float32)
    gate_z = projected[:, :inner_w].astype(jnp.bfloat16)
    mixed_in = projected[:, inner_w:].astype(jnp.bfloat16).reshape(frame_count, row_count, col_count, -1)
    step_raw = jnp.dot(flat_act, step_proj, preferred_element_type=jnp.float32) + step_bias
    step_sizes = jax.nn.softplus(step_raw).astype(jnp.bfloat16)
    padded = jnp.pad(mixed_in.astype(jnp.float32), ((0, 0), (1, 1), (1, 1), (0, 0)))
    before = conv_apply(padded, conv_kernel, conv_bias, row_count, col_count)
    activated = jax.nn.silu(before).astype(jnp.bfloat16)
    per_row = jnp.transpose(activated, (1, 0, 2, 3))
    steps_row = jnp.transpose(step_sizes.reshape(frame_count, row_count, col_count, head_count), (1, 0, 2, 3))

    def split_row(row_act):
        act_float = row_act.astype(jnp.float32)
        heads_in = act_float[..., :inner_w].reshape(frame_count, col_count, head_count, head_dim)
        return (heads_in, act_float[..., inner_w:inner_w + state_n], act_float[..., inner_w + state_n:])

    def forward_row(pieces):
        heads_in, b_proj, c_proj = split_row(pieces[0])
        result, _ = ssd_sequence(heads_in, b_proj, c_proj, pieces[1].astype(jnp.float32), decay_rates, skip_gain, FR_DEV)
        return result.astype(jnp.bfloat16)
    ssd_rows = lax.map(forward_row, (per_row, steps_row))
    ssd_out = jnp.transpose(ssd_rows, (1, 0, 2, 3, 4)).reshape(-1, inner_w)
    normed = gate_norm(ssd_out.astype(jnp.float32), gate_z.astype(jnp.float32), norm_gain).astype(jnp.bfloat16)
    layer_out = jnp.dot(normed, out_proj, preferred_element_type=jnp.float32).astype(jnp.bfloat16).reshape(activations.shape)
    contract_rows = (((0,), (0,)), ((), ()))
    contract_cols = (((1,), (1,)), ((), ()))
    cot_flat = out_cotangent.reshape(-1, model_width)
    d_normed = lax.dot_general(cot_flat, out_proj, contract_cols, preferred_element_type=jnp.float32)
    grad_out_proj_t = lax.dot_general(cot_flat, normed, contract_rows, preferred_element_type=jnp.float32)
    _, pull_norm = jax.vjp(gate_norm, ssd_out.astype(jnp.float32), gate_z.astype(jnp.float32), norm_gain)
    d_ssd, d_gate, grad_norm_gain = pull_norm(d_normed)
    d_ssd = d_ssd.astype(jnp.bfloat16)
    d_rows = jnp.transpose(d_ssd.reshape(frame_count, row_count, col_count, head_count, head_dim), (1, 0, 2, 3, 4))

    def backward_row(pieces):

        def ssd_local(heads_in, b_proj, c_proj, step_in, rate_in, gain_in):
            return ssd_sequence(heads_in, b_proj, c_proj, step_in, rate_in, gain_in, FR_DEV)
        heads_in, b_proj, c_proj = split_row(pieces[0])
        outputs, pull_back = jax.vjp(ssd_local, heads_in, b_proj, c_proj, pieces[1].astype(jnp.float32), decay_rates, skip_gain)
        gradients = pull_back((pieces[2].astype(jnp.float32), jnp.zeros_like(outputs[1])))
        d_act = jnp.concatenate([gradients[0].reshape(frame_count, col_count, inner_w), gradients[1], gradients[2]], axis=-1).astype(jnp.bfloat16)
        return (d_act, gradients[3].astype(jnp.bfloat16), gradients[4], gradients[5])
    d_act_rows, d_step_rows, rate_parts, gain_parts = lax.map(backward_row, (per_row, steps_row, d_rows))
    grad_decay_rates = lax.optimization_barrier(jnp.sum(rate_parts, axis=0))
    grad_skip_gain = lax.optimization_barrier(jnp.sum(gain_parts, axis=0))
    d_act = jnp.transpose(d_act_rows, (1, 0, 2, 3)).astype(jnp.float32)
    d_before = d_act * silu_slope(before)
    grad_conv_kernel = kernel_grad(d_before, padded, row_count, col_count)
    grad_conv_bias = lax.optimization_barrier(jnp.sum(d_before, axis=(0, 1, 2)))
    d_padded = jnp.pad(d_before, ((0, 0), (1, 1), (1, 1), (0, 0)))
    d_mixed = conv_transpose(d_padded, conv_kernel, row_count, col_count)
    d_steps = jnp.transpose(d_step_rows, (1, 0, 2, 3)).reshape(-1, head_count).astype(jnp.float32)
    d_raw = d_steps * jax.nn.sigmoid(step_raw)
    grad_step_bias = lax.optimization_barrier(jnp.sum(d_raw, axis=0))
    d_raw_half = d_raw.astype(jnp.bfloat16)
    d_projected = jnp.concatenate([d_gate, d_mixed.reshape(-1, d_mixed.shape[-1])], axis=1).astype(jnp.bfloat16)
    grad_input = (lax.dot_general(d_projected, in_proj, contract_cols, preferred_element_type=jnp.float32) + lax.dot_general(d_raw_half, step_proj, contract_cols, preferred_element_type=jnp.float32)).astype(jnp.bfloat16).reshape(activations.shape)
    grad_in_proj = lax.dot_general(flat_act, d_projected, contract_rows, preferred_element_type=jnp.float32)
    grad_step_proj = lax.dot_general(flat_act, d_raw_half, contract_rows, preferred_element_type=jnp.float32)
    return (layer_out, grad_input, grad_in_proj, grad_step_proj, grad_out_proj_t, grad_conv_kernel, grad_conv_bias, grad_step_bias, grad_decay_rates, grad_skip_gain, grad_norm_gain)
```

```python
import functools

import jax
import jax.numpy as jnp
from jax import lax
from jax.experimental import pallas as pl
from jax.experimental.pallas import tpu as pltpu
from jax.sharding import PartitionSpec as P

top_precision = lax.Precision.HIGHEST
norm_eps = 1e-05
LANES = 128
VMEM_BYTES = 40 * 1024 * 1024

contract_rows = (((0,), (0,)), ((), ()))
contract_cols = (((1,), (1,)), ((), ()))


def dot_f32(left, right, dims=(((1,), (0,)), ((), ()))):
    return lax.dot_general(left, right, dims, preferred_element_type=jnp.float32)


def half(value):
    return value.astype(jnp.bfloat16)


def whole_call(body, out_shape, scratch=()):
    return pl.pallas_call(
        body,
        out_shape=out_shape,
        scratch_shapes=scratch,
        compiler_params=pltpu.CompilerParams(vmem_limit_bytes=VMEM_BYTES),
    )


def ssd_kernel(
    few,
    act_ref,
    gate_ref,
    d_normed_ref,
    run_ref,
    run_t_ref,
    step_t_ref,
    skip_ref,
    norm_gain_ref,
    normed_ref,
    d_gate_ref,
    d_act_ref,
    row_ref,
    col_ref,
    skip_part_ref,
    norm_part_ref,
    decay_ref,
    ssd_ref,
    d_ssd_ref,
):
    count = act_ref.shape[0]
    inner_w = gate_ref.shape[1]
    heads = run_ref.shape[1]
    head_dim = inner_w // heads
    per_tile = LANES // head_dim
    rows = lax.broadcasted_iota(jnp.int32, (count, count), 0)
    cols = lax.broadcasted_iota(jnp.int32, (count, count), 1)
    causal = (lax.rem(rows, few) == lax.rem(cols, few)) & (rows >= cols)
    lane = lax.broadcasted_iota(jnp.int32, (count, LANES), 1)
    low = lane < head_dim
    bc = act_ref[:, inner_w:]
    swapped_float = pltpu.roll(bc.astype(jnp.float32), head_dim, 1)
    swapped = half(swapped_float)
    inner_cb = dot_f32(half(jnp.where(low, swapped_float, 0.0)), bc, contract_cols)
    inner_cb = jnp.where(causal, inner_cb, 0.0)

    for tile in range(inner_w // LANES):
        span = slice(tile * LANES, (tile + 1) * LANES)
        u = act_ref[:, span]
        result = u.astype(jnp.float32) * skip_ref[:, span]
        for place in range(per_tile):
            h = tile * per_tile + place
            spread = run_t_ref[h : h + 1, :] - run_ref[:, h : h + 1]
            decay = jnp.exp(jnp.where(causal, spread, 0.0))
            decay_ref[h] = decay
            weights = half(inner_cb * decay * step_t_ref[h : h + 1, :])
            mine = lane // head_dim == place
            result = result + jnp.where(mine, dot_f32(weights, u), 0.0)
        ssd_ref[:, span] = half(result)

    squares = jnp.zeros((count, LANES), jnp.float32)
    crossed = jnp.zeros((count, LANES), jnp.float32)
    for tile in range(inner_w // LANES):
        span = slice(tile * LANES, (tile + 1) * LANES)
        gate = gate_ref[:, span].astype(jnp.float32)
        gated = ssd_ref[:, span].astype(jnp.float32) * (gate * jax.nn.sigmoid(gate))
        squares = squares + gated * gated
        crossed = crossed + gated * (d_normed_ref[:, span] * norm_gain_ref[:, span])
    mean_square = jnp.sum(squares, axis=1, keepdims=True) / inner_w
    scale_row = lax.rsqrt(mean_square + norm_eps)
    pulled = jnp.sum(crossed, axis=1, keepdims=True) / inner_w * scale_row * scale_row
    for tile in range(inner_w // LANES):
        span = slice(tile * LANES, (tile + 1) * LANES)
        gate = gate_ref[:, span].astype(jnp.float32)
        squashed = jax.nn.sigmoid(gate)
        silu = gate * squashed
        ssd = ssd_ref[:, span].astype(jnp.float32)
        gated = ssd * silu
        scaled = gated * scale_row
        d_normed = d_normed_ref[:, span]
        normed_ref[:, span] = half(scaled * norm_gain_ref[:, span])
        norm_part_ref[:, span] = jnp.sum(d_normed * scaled, axis=0, keepdims=True)
        d_gated = scale_row * (d_normed * norm_gain_ref[:, span] - gated * pulled)
        d_ssd_ref[:, span] = half(d_gated * silu)
        d_gate_ref[:, span] = half(d_gated * ssd * (squashed * (1.0 + gate * (1.0 - squashed))))

    d_cb = jnp.zeros((count, count), jnp.float32)
    for tile in range(inner_w // LANES):
        span = slice(tile * LANES, (tile + 1) * LANES)
        u = act_ref[:, span]
        d_y = d_ssd_ref[:, span]
        d_y_float = d_y.astype(jnp.float32)
        d_u = d_y_float * skip_ref[:, span]
        skip_part_ref[:, span] = jnp.sum(d_y_float * u.astype(jnp.float32), axis=0, keepdims=True)
        for place in range(per_tile):
            h = tile * per_tile + place
            mine = lane // head_dim == place
            d_weights = dot_f32(half(jnp.where(mine, d_y_float, 0.0)), u, contract_cols)
            decay = decay_ref[h]
            step_row = step_t_ref[h : h + 1, :]
            d_scaled = d_weights * decay
            d_cb = d_cb + d_scaled * step_row
            product = d_scaled * inner_cb
            col_ref[h : h + 1, :] = jnp.sum(product, axis=0, keepdims=True)
            row_ref[:, h : h + 1] = jnp.sum(product * step_row, axis=1, keepdims=True)
            weights = half(inner_cb * decay * step_row)
            d_u = d_u + jnp.where(mine, dot_f32(weights, d_y, contract_rows), 0.0)
        d_act_ref[:, span] = half(d_u)
    d_cb = half(jnp.where(causal, d_cb, 0.0))
    d_act_ref[:, inner_w:] = half(
        jnp.where(low, dot_f32(d_cb, swapped, contract_rows), dot_f32(d_cb, swapped))
    )


def sideways(flat, cols):
    rows = flat.shape[0]
    col = lax.rem(lax.broadcasted_iota(jnp.int32, flat.shape, 0), cols)
    left = jnp.where(col > 0, pltpu.roll(flat, 1, 0), 0.0)
    right = jnp.where(col < cols - 1, pltpu.roll(flat, rows - 1, 0), 0.0)
    return left, flat, right


def tall_tile(low_ref, mid_ref, high_ref, span):
    stacked = jnp.concatenate(
        [ref[:, :, :, span].astype(jnp.float32) for ref in (low_ref, mid_ref, high_ref)], axis=1
    )
    return stacked, stacked.reshape(-1, stacked.shape[-1])


def conv_kernel_body(low_ref, mid_ref, high_ref, kernel_ref, bias_ref, before_ref, act_ref):
    row_count, cols = mid_ref.shape[1], mid_ref.shape[2]
    for tile in range(mid_ref.shape[3] // LANES):
        span = slice(tile * LANES, (tile + 1) * LANES)
        stacked, flat = tall_tile(low_ref, mid_ref, high_ref, span)
        total = bias_ref[:, span].reshape(1, 1, 1, -1)
        for col_off, moved in enumerate(sideways(flat, cols)):
            moved = moved.reshape(stacked.shape)
            for row_off in range(3):
                k = 3 * row_off + col_off
                tap = kernel_ref[k : k + 1, span].reshape(1, 1, 1, -1)
                total = total + tap * moved[:, row_off : row_off + row_count]
        before_ref[:, :, :, span] = total
        act_ref[:, :, :, span] = half(total * jax.nn.sigmoid(total))


def d_before_body(d_act_ref, before_ref, d_before_ref, d_half_ref):
    for tile in range(before_ref.shape[3] // LANES):
        span = slice(tile * LANES, (tile + 1) * LANES)
        before = before_ref[:, :, :, span]
        squashed = jax.nn.sigmoid(before)
        slope = squashed * (1.0 + before * (1.0 - squashed))
        d_before = d_act_ref[:, :, :, span].astype(jnp.float32) * slope
        d_before_ref[:, :, :, span] = d_before
        d_half_ref[:, :, :, span] = half(d_before)


def kernel_grad_body(low_ref, mid_ref, high_ref, d_before_ref, part_ref):
    row_count, cols = mid_ref.shape[1], mid_ref.shape[2]
    for tile in range(mid_ref.shape[3] // LANES):
        span = slice(tile * LANES, (tile + 1) * LANES)
        stacked, flat = tall_tile(low_ref, mid_ref, high_ref, span)
        d_before = d_before_ref[:, :, :, span]
        for col_off, moved in enumerate(sideways(flat, cols)):
            moved = moved.reshape(stacked.shape)
            for row_off in range(3):
                product = d_before * moved[:, row_off : row_off + row_count]
                k = 3 * row_off + col_off
                part_ref[k : k + 1, span] = jnp.sum(
                    product.reshape(-1, LANES), axis=0, keepdims=True
                )
        part_ref[9:10, span] = jnp.sum(d_before.reshape(-1, LANES), axis=0, keepdims=True)


def d_mixed_body(low_ref, mid_ref, high_ref, kernel_ref, d_mixed_ref):
    row_count, cols = mid_ref.shape[1], mid_ref.shape[2]
    for tile in range(mid_ref.shape[3] // LANES):
        span = slice(tile * LANES, (tile + 1) * LANES)
        stacked, flat = tall_tile(low_ref, mid_ref, high_ref, span)
        total = jnp.zeros(mid_ref.shape[:3] + (LANES,), jnp.float32)
        for shift, moved in enumerate(sideways(flat, cols)):
            moved = moved.reshape(stacked.shape)
            for row_off in range(3):
                k = 3 * row_off + 2 - shift
                tap = kernel_ref[k : k + 1, span].reshape(1, 1, 1, -1)
                total = total + tap * moved[:, 2 - row_off : 2 - row_off + row_count]
        d_mixed_ref[:, :, :, span] = half(total)


def edges(block):
    count = lax.axis_size("space")
    forward = [(i, i + 1) for i in range(count - 1)]
    backward = [(i + 1, i) for i in range(count - 1)]
    low = lax.ppermute(block[:, -1:], "space", forward)
    high = lax.ppermute(block[:, :1], "space", backward)
    return low, high


def to_sequences(block):
    parts = lax.axis_size("tm")
    frames, tokens, width = block.shape
    few = tokens // parts
    sent = block.reshape(frames, parts, few, width).transpose(1, 0, 2, 3)
    sent = sent.reshape(parts, frames * few, width)
    got = lax.all_to_all(sent, "tm", split_axis=0, concat_axis=0, tiled=True)
    return got.reshape(parts * frames * few, width)


def to_frames(flat, frames):
    parts = lax.axis_size("tm")
    few = flat.shape[0] // (parts * frames)
    width = flat.shape[1]
    got = lax.all_to_all(
        flat.reshape(parts, frames * few, width), "tm", split_axis=0, concat_axis=0, tiled=True
    )
    got = got.reshape(parts, frames, few, width).transpose(1, 0, 2, 3)
    return got.reshape(frames, parts * few, width)


def scatter_sum(partial):
    return lax.psum_scatter(
        half(partial), ("tm", "space"), scatter_dimension=0, tiled=True
    ).astype(jnp.float32)


def on_device(
    activations,
    in_proj,
    step_proj,
    step_bias,
    decay_rates,
    conv_kernel,
    conv_bias,
    skip_gain,
    norm_gain,
    out_proj,
    out_cotangent,
):
    frame_count, row_count, col_count, model_width = activations.shape
    inner_w = out_proj.shape[0]
    head_count = step_proj.shape[1]
    head_dim = inner_w // head_count
    conv_w = in_proj.shape[1] - inner_w
    token_count = row_count * col_count
    few = token_count // lax.axis_size("tm")
    grid = (frame_count, row_count, col_count)

    flat_act = activations.reshape(-1, model_width)
    mixed_in = half(dot_f32(flat_act, in_proj[:, inner_w:])).reshape(grid + (conv_w,))
    low, high = edges(mixed_in)
    both = jnp.concatenate([activations, out_cotangent], axis=-1)
    both_seq = to_sequences(both.reshape(frame_count, token_count, -1))
    flat_kernel = conv_kernel.reshape(9, conv_w)
    before, activated = whole_call(
        conv_kernel_body,
        (
            jax.ShapeDtypeStruct(grid + (conv_w,), jnp.float32),
            jax.ShapeDtypeStruct(grid + (conv_w,), jnp.bfloat16),
        ),
    )(low, mixed_in, high, flat_kernel, conv_bias.reshape(1, -1))
    act_seq = to_sequences(activated.reshape(frame_count, token_count, conv_w))

    x_seq, cot_seq = both_seq[:, :model_width], both_seq[:, model_width:]
    count = x_seq.shape[0]
    gate_z = half(dot_f32(x_seq, in_proj[:, :inner_w]))
    step_raw = dot_f32(x_seq, step_proj) + step_bias
    steps = half(jax.nn.softplus(step_raw)).astype(jnp.float32)
    d_normed = dot_f32(cot_seq, out_proj, contract_cols)
    index = jnp.arange(count)
    earlier = (
        (index[:, None] % few == index[None, :] % few) & (index[:, None] >= index[None, :])
    ).astype(jnp.float32)
    running = jnp.dot(earlier, steps * decay_rates, precision=top_precision)
    f32, bf16 = jnp.float32, jnp.bfloat16
    normed, d_gate, d_act_seq, row_sums, col_sums, skip_part, norm_part = whole_call(
        functools.partial(ssd_kernel, few),
        (
            jax.ShapeDtypeStruct((count, inner_w), bf16),
            jax.ShapeDtypeStruct((count, inner_w), bf16),
            jax.ShapeDtypeStruct((count, conv_w), bf16),
            jax.ShapeDtypeStruct((count, head_count), f32),
            jax.ShapeDtypeStruct((head_count, count), f32),
            jax.ShapeDtypeStruct((1, inner_w), f32),
            jax.ShapeDtypeStruct((1, inner_w), f32),
        ),
        (
            pltpu.VMEM((head_count, count, count), f32),
            pltpu.VMEM((count, inner_w), bf16),
            pltpu.VMEM((count, inner_w), bf16),
        ),
    )(
        act_seq,
        gate_z,
        d_normed,
        running,
        running.T,
        steps.T,
        jnp.repeat(skip_gain, head_dim).reshape(1, -1),
        norm_gain.reshape(1, -1),
    )
    d_act = to_frames(d_act_seq, frame_count).reshape(grid + (conv_w,))
    layer_seq = half(dot_f32(normed, out_proj))
    col_turned = col_sums.T
    d_running = col_turned * steps - row_sums
    d_decay = jnp.dot(earlier.T, d_running, precision=top_precision)
    d_steps = half(col_turned + d_decay * decay_rates).astype(f32)
    rate_part = jnp.sum(d_decay * steps, axis=0)
    gain_part = jnp.sum(skip_part.reshape(head_count, head_dim), axis=1)
    d_raw = d_steps * jax.nn.sigmoid(step_raw)
    bias_part = jnp.sum(d_raw, axis=0)
    d_raw_half = half(d_raw)
    back = to_frames(jnp.concatenate([d_gate, layer_seq, d_raw_half], axis=1), frame_count)
    back = back.reshape(-1, back.shape[-1])
    early = scatter_sum(
        jnp.concatenate(
            [
                dot_f32(x_seq, d_gate, contract_rows),
                dot_f32(cot_seq, normed, contract_rows),
                dot_f32(x_seq, d_raw_half, contract_rows),
            ],
            axis=1,
        )
    )

    d_before, d_half = whole_call(
        d_before_body,
        (
            jax.ShapeDtypeStruct(before.shape, f32),
            jax.ShapeDtypeStruct(before.shape, bf16),
        ),
    )(d_act, before)
    d_low, d_high = edges(d_half)
    conv_parts = whole_call(kernel_grad_body, jax.ShapeDtypeStruct((10, conv_w), f32))(
        low, mixed_in, high, d_before
    )
    d_mixed = whole_call(d_mixed_body, jax.ShapeDtypeStruct(before.shape, bf16))(
        d_low, d_before, d_high, flat_kernel
    ).reshape(-1, conv_w)
    late = scatter_sum(dot_f32(flat_act, d_mixed, contract_rows))
    d_gate_frames = back[:, :inner_w]
    layer_out = back[:, inner_w : 2 * inner_w].reshape(activations.shape)
    d_raw_frames = back[:, 2 * inner_w :]
    grad_input = half(
        dot_f32(d_gate_frames, in_proj[:, :inner_w], contract_cols)
        + dot_f32(d_mixed, in_proj[:, inner_w:], contract_cols)
        + dot_f32(d_raw_frames, step_proj, contract_cols)
    ).reshape(activations.shape)
    grad_in_proj = jnp.concatenate([early[:, :inner_w], late], axis=1)
    grad_out_proj_t = early[:, inner_w : 2 * inner_w]
    grad_step_proj = early[:, 2 * inner_w :]
    small = jnp.concatenate(
        [conv_parts.reshape(-1), norm_part.reshape(-1), bias_part, rate_part, gain_part]
    )
    small = lax.psum(small, ("tm", "space"))
    taps = 9 * conv_w
    sizes = [taps, conv_w, inner_w, head_count, head_count, head_count]
    pieces, start = [], 0
    for size in sizes:
        pieces.append(small[start : start + size])
        start += size
    return (
        layer_out,
        grad_input,
        grad_in_proj,
        grad_step_proj,
        grad_out_proj_t,
        pieces[0].reshape(3, 3, conv_w),
        pieces[1],
        pieces[3],
        pieces[4],
        pieces[5],
        pieces[2],
    )


def solution(mesh):
    placed = (
        P("tm", "space", None, None),
        P(),
        P(),
        P(),
        P(),
        P(),
        P(),
        P(),
        P(),
        P(),
        P("tm", "space", None, None),
    )
    return jax.shard_map(
        on_device,
        mesh=mesh,
        in_specs=placed,
        out_specs=(
            P("tm", "space", None, None),
            P("tm", "space", None, None),
            P(("tm", "space"), None),
            P(("tm", "space"), None),
            P(("tm", "space"), None),
            P(),
            P(),
            P(),
            P(),
            P(),
            P(),
        ),
        check_vma=False,
    )
```

```python
import functools

import jax
import jax.numpy as jnp
from jax import lax
from jax.experimental import pallas as pl
from jax.experimental.pallas import tpu as pltpu
from jax.sharding import PartitionSpec as P

top_precision = lax.Precision.HIGHEST
norm_eps = 1e-05
LANES = 128
VMEM_BYTES = 40 * 1024 * 1024

contract_rows = (((0,), (0,)), ((), ()))
contract_cols = (((1,), (1,)), ((), ()))


def dot_f32(left, right, dims=(((1,), (0,)), ((), ()))):
    return lax.dot_general(left, right, dims, preferred_element_type=jnp.float32)


def half(value):
    return value.astype(jnp.bfloat16)


def whole_call(body, out_shape, scratch=()):
    return pl.pallas_call(
        body,
        out_shape=out_shape,
        scratch_shapes=scratch,
        compiler_params=pltpu.CompilerParams(vmem_limit_bytes=VMEM_BYTES),
    )


def ssd_kernel(
    few,
    act_ref,
    gate_ref,
    d_normed_ref,
    run_ref,
    run_t_ref,
    step_t_ref,
    skip_ref,
    norm_gain_ref,
    normed_ref,
    d_gate_ref,
    d_act_ref,
    row_ref,
    col_ref,
    skip_part_ref,
    norm_part_ref,
    decay_ref,
    ssd_ref,
    d_ssd_ref,
):
    count = act_ref.shape[0]
    inner_w = gate_ref.shape[1]
    heads = run_ref.shape[1]
    head_dim = inner_w // heads
    per_tile = LANES // head_dim
    rows = lax.broadcasted_iota(jnp.int32, (count, count), 0)
    cols = lax.broadcasted_iota(jnp.int32, (count, count), 1)
    causal = (lax.rem(rows, few) == lax.rem(cols, few)) & (rows >= cols)
    lane = lax.broadcasted_iota(jnp.int32, (count, LANES), 1)
    low = lane < head_dim
    bc = act_ref[:, inner_w:]
    swapped_float = pltpu.roll(bc.astype(jnp.float32), head_dim, 1)
    swapped = half(swapped_float)
    inner_cb = dot_f32(half(jnp.where(low, swapped_float, 0.0)), bc, contract_cols)
    inner_cb = jnp.where(causal, inner_cb, 0.0)

    for tile in range(inner_w // LANES):
        span = slice(tile * LANES, (tile + 1) * LANES)
        u = act_ref[:, span]
        result = u.astype(jnp.float32) * skip_ref[:, span]
        for place in range(per_tile):
            h = tile * per_tile + place
            spread = run_t_ref[h : h + 1, :] - run_ref[:, h : h + 1]
            decay = jnp.exp(jnp.where(causal, spread, 0.0))
            decay_ref[h] = decay
            weights = half(inner_cb * decay * step_t_ref[h : h + 1, :])
            mine = lane // head_dim == place
            result = result + jnp.where(mine, dot_f32(weights, u), 0.0)
        ssd_ref[:, span] = half(result)

    squares = jnp.zeros((count, LANES), jnp.float32)
    crossed = jnp.zeros((count, LANES), jnp.float32)
    for tile in range(inner_w // LANES):
        span = slice(tile * LANES, (tile + 1) * LANES)
        gate = gate_ref[:, span].astype(jnp.float32)
        gated = ssd_ref[:, span].astype(jnp.float32) * (gate * jax.nn.sigmoid(gate))
        squares = squares + gated * gated
        crossed = crossed + gated * (d_normed_ref[:, span] * norm_gain_ref[:, span])
    mean_square = jnp.sum(squares, axis=1, keepdims=True) / inner_w
    scale_row = lax.rsqrt(mean_square + norm_eps)
    pulled = jnp.sum(crossed, axis=1, keepdims=True) / inner_w * scale_row * scale_row
    for tile in range(inner_w // LANES):
        span = slice(tile * LANES, (tile + 1) * LANES)
        gate = gate_ref[:, span].astype(jnp.float32)
        squashed = jax.nn.sigmoid(gate)
        silu = gate * squashed
        ssd = ssd_ref[:, span].astype(jnp.float32)
        gated = ssd * silu
        scaled = gated * scale_row
        d_normed = d_normed_ref[:, span]
        normed_ref[:, span] = half(scaled * norm_gain_ref[:, span])
        norm_part_ref[:, span] = jnp.sum(d_normed * scaled, axis=0, keepdims=True)
        d_gated = scale_row * (d_normed * norm_gain_ref[:, span] - gated * pulled)
        d_ssd_ref[:, span] = half(d_gated * silu)
        d_gate_ref[:, span] = half(d_gated * ssd * (squashed * (1.0 + gate * (1.0 - squashed))))

    d_cb = jnp.zeros((count, count), jnp.float32)
    for tile in range(inner_w // LANES):
        span = slice(tile * LANES, (tile + 1) * LANES)
        u = act_ref[:, span]
        d_y = d_ssd_ref[:, span]
        d_y_float = d_y.astype(jnp.float32)
        d_u = d_y_float * skip_ref[:, span]
        skip_part_ref[:, span] = jnp.sum(d_y_float * u.astype(jnp.float32), axis=0, keepdims=True)
        for place in range(per_tile):
            h = tile * per_tile + place
            mine = lane // head_dim == place
            d_weights = dot_f32(half(jnp.where(mine, d_y_float, 0.0)), u, contract_cols)
            decay = decay_ref[h]
            step_row = step_t_ref[h : h + 1, :]
            d_scaled = d_weights * decay
            d_cb = d_cb + d_scaled * step_row
            product = d_scaled * inner_cb
            col_ref[h : h + 1, :] = jnp.sum(product, axis=0, keepdims=True)
            row_ref[:, h : h + 1] = jnp.sum(product * step_row, axis=1, keepdims=True)
            weights = half(inner_cb * decay * step_row)
            d_u = d_u + jnp.where(mine, dot_f32(weights, d_y, contract_rows), 0.0)
        d_act_ref[:, span] = half(d_u)
    d_cb = half(jnp.where(causal, d_cb, 0.0))
    d_act_ref[:, inner_w:] = half(
        jnp.where(low, dot_f32(d_cb, swapped, contract_rows), dot_f32(d_cb, swapped))
    )


def sideways(flat, cols):
    rows = flat.shape[0]
    col = lax.rem(lax.broadcasted_iota(jnp.int32, flat.shape, 0), cols)
    left = jnp.where(col > 0, pltpu.roll(flat, 1, 0), 0.0)
    right = jnp.where(col < cols - 1, pltpu.roll(flat, rows - 1, 0), 0.0)
    return left, flat, right


def tall_tile(low_ref, mid_ref, high_ref, span):
    stacked = jnp.concatenate(
        [ref[:, :, :, span].astype(jnp.float32) for ref in (low_ref, mid_ref, high_ref)], axis=1
    )
    return stacked, stacked.reshape(-1, stacked.shape[-1])


def conv_kernel_body(low_ref, mid_ref, high_ref, kernel_ref, bias_ref, before_ref, act_ref):
    row_count, cols = mid_ref.shape[1], mid_ref.shape[2]
    for tile in range(mid_ref.shape[3] // LANES):
        span = slice(tile * LANES, (tile + 1) * LANES)
        stacked, flat = tall_tile(low_ref, mid_ref, high_ref, span)
        total = bias_ref[:, span].reshape(1, 1, 1, -1)
        for col_off, moved in enumerate(sideways(flat, cols)):
            moved = moved.reshape(stacked.shape)
            for row_off in range(3):
                k = 3 * row_off + col_off
                tap = kernel_ref[k : k + 1, span].reshape(1, 1, 1, -1)
                total = total + tap * moved[:, row_off : row_off + row_count]
        before_ref[:, :, :, span] = total
        act_ref[:, :, :, span] = half(total * jax.nn.sigmoid(total))


def d_before_body(d_act_ref, before_ref, d_before_ref, d_half_ref):
    for tile in range(before_ref.shape[3] // LANES):
        span = slice(tile * LANES, (tile + 1) * LANES)
        before = before_ref[:, :, :, span]
        squashed = jax.nn.sigmoid(before)
        slope = squashed * (1.0 + before * (1.0 - squashed))
        d_before = d_act_ref[:, :, :, span].astype(jnp.float32) * slope
        d_before_ref[:, :, :, span] = d_before
        d_half_ref[:, :, :, span] = half(d_before)


def kernel_grad_body(low_ref, mid_ref, high_ref, d_before_ref, part_ref):
    row_count, cols = mid_ref.shape[1], mid_ref.shape[2]
    for tile in range(mid_ref.shape[3] // LANES):
        span = slice(tile * LANES, (tile + 1) * LANES)
        stacked, flat = tall_tile(low_ref, mid_ref, high_ref, span)
        d_before = d_before_ref[:, :, :, span]
        for col_off, moved in enumerate(sideways(flat, cols)):
            moved = moved.reshape(stacked.shape)
            for row_off in range(3):
                product = d_before * moved[:, row_off : row_off + row_count]
                k = 3 * row_off + col_off
                part_ref[k : k + 1, span] = jnp.sum(
                    product.reshape(-1, LANES), axis=0, keepdims=True
                )
        part_ref[9:10, span] = jnp.sum(d_before.reshape(-1, LANES), axis=0, keepdims=True)


def d_mixed_body(low_ref, mid_ref, high_ref, kernel_ref, d_mixed_ref):
    row_count, cols = mid_ref.shape[1], mid_ref.shape[2]
    for tile in range(mid_ref.shape[3] // LANES):
        span = slice(tile * LANES, (tile + 1) * LANES)
        stacked, flat = tall_tile(low_ref, mid_ref, high_ref, span)
        total = jnp.zeros(mid_ref.shape[:3] + (LANES,), jnp.float32)
        for shift, moved in enumerate(sideways(flat, cols)):
            moved = moved.reshape(stacked.shape)
            for row_off in range(3):
                k = 3 * row_off + 2 - shift
                tap = kernel_ref[k : k + 1, span].reshape(1, 1, 1, -1)
                total = total + tap * moved[:, 2 - row_off : 2 - row_off + row_count]
        d_mixed_ref[:, :, :, span] = half(total)


def edges(block):
    count = lax.axis_size("space")
    forward = [(i, i + 1) for i in range(count - 1)]
    backward = [(i + 1, i) for i in range(count - 1)]
    low = lax.ppermute(block[:, -1:], "space", forward)
    high = lax.ppermute(block[:, :1], "space", backward)
    return low, high


def to_sequences(block):
    parts = lax.axis_size("tm")
    frames, tokens, width = block.shape
    few = tokens // parts
    sent = block.reshape(frames, parts, few, width).transpose(1, 0, 2, 3)
    sent = sent.reshape(parts, frames * few, width)
    got = lax.all_to_all(sent, "tm", split_axis=0, concat_axis=0, tiled=True)
    return got.reshape(parts * frames * few, width)


def to_frames(flat, frames):
    parts = lax.axis_size("tm")
    few = flat.shape[0] // (parts * frames)
    width = flat.shape[1]
    got = lax.all_to_all(
        flat.reshape(parts, frames * few, width), "tm", split_axis=0, concat_axis=0, tiled=True
    )
    got = got.reshape(parts, frames, few, width).transpose(1, 0, 2, 3)
    return got.reshape(frames, parts * few, width)


def swapped_over(block, axis, bit):
    pairs = [(i, i ^ (1 << bit)) for i in range(lax.axis_size(axis))]
    return lax.ppermute(block, axis, pairs)


def halve(block, dim, axis, bit):
    mine = lax.rem(lax.axis_index(axis) // (1 << bit), 2)
    sent = half(lax.dynamic_index_in_dim(block, 1 - mine, dim, keepdims=False))
    kept = lax.dynamic_index_in_dim(block, mine, dim, keepdims=False)
    return kept + swapped_over(sent, axis, bit).astype(jnp.float32)


def bits_of(axis):
    return lax.axis_size(axis).bit_length() - 1


def scatter_sum(first, second):
    tm_bits, space_bits = bits_of("tm"), bits_of("space")
    devices = 1 << (tm_bits + space_bits)

    def split(block):
        block = block.reshape(
            (2,) * (tm_bits + space_bits) + (block.shape[0] // devices, block.shape[1])
        )
        return halve(block, tm_bits + space_bits - 1, "space", 0)

    first, second = split(first), split(second)
    for step in range(tm_bits):
        first = halve(first, tm_bits - 1 - step, "tm", step)
        second = halve(second, 0, "tm", tm_bits - 1 - step)
    joined = jnp.concatenate([first, second], axis=-1)
    for bit in range(1, space_bits):
        joined = halve(joined, space_bits - 1 - bit, "space", bit)
    return joined


def sum_everywhere(block):
    for axis in ("space", "tm"):
        for bit in range(bits_of(axis)):
            block = block + swapped_over(block, axis, bit)
    return block


def on_device(
    activations,
    in_proj,
    step_proj,
    step_bias,
    decay_rates,
    conv_kernel,
    conv_bias,
    skip_gain,
    norm_gain,
    out_proj,
    out_cotangent,
):
    frame_count, row_count, col_count, model_width = activations.shape
    inner_w = out_proj.shape[0]
    head_count = step_proj.shape[1]
    head_dim = inner_w // head_count
    conv_w = in_proj.shape[1] - inner_w
    token_count = row_count * col_count
    few = token_count // lax.axis_size("tm")
    grid = (frame_count, row_count, col_count)

    flat_act = activations.reshape(-1, model_width)
    mixed_in = half(dot_f32(flat_act, in_proj[:, inner_w:])).reshape(grid + (conv_w,))
    low, high = edges(mixed_in)
    both = jnp.concatenate([activations, out_cotangent], axis=-1)
    both_seq = to_sequences(both.reshape(frame_count, token_count, -1))
    flat_kernel = conv_kernel.reshape(9, conv_w)
    before, activated = whole_call(
        conv_kernel_body,
        (
            jax.ShapeDtypeStruct(grid + (conv_w,), jnp.float32),
            jax.ShapeDtypeStruct(grid + (conv_w,), jnp.bfloat16),
        ),
    )(low, mixed_in, high, flat_kernel, conv_bias.reshape(1, -1))
    act_seq = to_sequences(activated.reshape(frame_count, token_count, conv_w))

    x_seq, cot_seq = both_seq[:, :model_width], both_seq[:, model_width:]
    count = x_seq.shape[0]
    gate_z = half(dot_f32(x_seq, in_proj[:, :inner_w]))
    step_raw = dot_f32(x_seq, step_proj) + step_bias
    steps = half(jax.nn.softplus(step_raw)).astype(jnp.float32)
    d_normed = dot_f32(cot_seq, out_proj, contract_cols)
    index = jnp.arange(count)
    earlier = (
        (index[:, None] % few == index[None, :] % few) & (index[:, None] >= index[None, :])
    ).astype(jnp.float32)
    running = jnp.dot(earlier, steps * decay_rates, precision=top_precision)
    f32, bf16 = jnp.float32, jnp.bfloat16
    normed, d_gate, d_act_seq, row_sums, col_sums, skip_part, norm_part = whole_call(
        functools.partial(ssd_kernel, few),
        (
            jax.ShapeDtypeStruct((count, inner_w), bf16),
            jax.ShapeDtypeStruct((count, inner_w), bf16),
            jax.ShapeDtypeStruct((count, conv_w), bf16),
            jax.ShapeDtypeStruct((count, head_count), f32),
            jax.ShapeDtypeStruct((head_count, count), f32),
            jax.ShapeDtypeStruct((1, inner_w), f32),
            jax.ShapeDtypeStruct((1, inner_w), f32),
        ),
        (
            pltpu.VMEM((head_count, count, count), f32),
            pltpu.VMEM((count, inner_w), bf16),
            pltpu.VMEM((count, inner_w), bf16),
        ),
    )(
        act_seq,
        gate_z,
        d_normed,
        running,
        running.T,
        steps.T,
        jnp.repeat(skip_gain, head_dim).reshape(1, -1),
        norm_gain.reshape(1, -1),
    )
    d_act = to_frames(d_act_seq, frame_count).reshape(grid + (conv_w,))
    layer_seq = half(dot_f32(normed, out_proj))
    col_turned = col_sums.T
    d_running = col_turned * steps - row_sums
    d_decay = jnp.dot(earlier.T, d_running, precision=top_precision)
    d_steps = half(col_turned + d_decay * decay_rates).astype(f32)
    rate_part = jnp.sum(d_decay * steps, axis=0)
    gain_part = jnp.sum(skip_part.reshape(head_count, head_dim), axis=1)
    d_raw = d_steps * jax.nn.sigmoid(step_raw)
    bias_part = jnp.sum(d_raw, axis=0)
    d_raw_half = half(d_raw)
    back = to_frames(jnp.concatenate([d_gate, layer_seq, d_raw_half], axis=1), frame_count)
    back = back.reshape(-1, back.shape[-1])
    early = scatter_sum(
        dot_f32(x_seq, jnp.concatenate([d_gate, d_raw_half], axis=1), contract_rows),
        dot_f32(cot_seq, normed, contract_rows),
    )

    d_before, d_half = whole_call(
        d_before_body,
        (
            jax.ShapeDtypeStruct(before.shape, f32),
            jax.ShapeDtypeStruct(before.shape, bf16),
        ),
    )(d_act, before)
    d_low, d_high = edges(d_half)
    conv_parts = whole_call(kernel_grad_body, jax.ShapeDtypeStruct((10, conv_w), f32))(
        low, mixed_in, high, d_before
    )
    d_mixed = whole_call(d_mixed_body, jax.ShapeDtypeStruct(before.shape, bf16))(
        d_low, d_before, d_high, flat_kernel
    ).reshape(-1, conv_w)
    cut = conv_w // (2 * LANES) * LANES
    late = scatter_sum(
        dot_f32(flat_act, d_mixed[:, :cut], contract_rows),
        dot_f32(flat_act, d_mixed[:, cut:], contract_rows),
    )
    d_gate_frames = back[:, :inner_w]
    layer_out = back[:, inner_w : 2 * inner_w].reshape(activations.shape)
    d_raw_frames = back[:, 2 * inner_w :]
    grad_input = half(
        dot_f32(d_gate_frames, in_proj[:, :inner_w], contract_cols)
        + dot_f32(d_mixed, in_proj[:, inner_w:], contract_cols)
        + dot_f32(d_raw_frames, step_proj, contract_cols)
    ).reshape(activations.shape)
    grad_in_proj = jnp.concatenate([early[:, :inner_w], late], axis=1)
    grad_step_proj = early[:, inner_w : inner_w + head_count]
    grad_out_proj_t = early[:, inner_w + head_count :]
    small = jnp.concatenate(
        [conv_parts.reshape(-1), norm_part.reshape(-1), bias_part, rate_part, gain_part]
    )
    small = sum_everywhere(small)
    taps = 9 * conv_w
    sizes = [taps, conv_w, inner_w, head_count, head_count, head_count]
    pieces, start = [], 0
    for size in sizes:
        pieces.append(small[start : start + size])
        start += size
    return (
        layer_out,
        grad_input,
        grad_in_proj,
        grad_step_proj,
        grad_out_proj_t,
        pieces[0].reshape(3, 3, conv_w),
        pieces[1],
        pieces[3],
        pieces[4],
        pieces[5],
        pieces[2],
    )


def solution(mesh):
    placed = (
        P("tm", "space", None, None),
        P(),
        P(),
        P(),
        P(),
        P(),
        P(),
        P(),
        P(),
        P(),
        P("tm", "space", None, None),
    )
    return jax.shard_map(
        on_device,
        mesh=mesh,
        in_specs=placed,
        out_specs=(
            P("tm", "space", None, None),
            P("tm", "space", None, None),
            P(("tm", "space"), None),
            P(("tm", "space"), None),
            P(("tm", "space"), None),
            P(),
            P(),
            P(),
            P(),
            P(),
            P(),
        ),
        check_vma=False,
    )
```

```python
import functools

import jax
import jax.numpy as jnp
from jax import lax
from jax.experimental import pallas as pl
from jax.experimental.pallas import tpu as pltpu
from jax.sharding import PartitionSpec as P

top_precision = lax.Precision.HIGHEST
norm_eps = 1e-05
LANES = 128
VMEM_BYTES = 40 * 1024 * 1024

contract_rows = (((0,), (0,)), ((), ()))
contract_cols = (((1,), (1,)), ((), ()))


def dot_f32(left, right, dims=(((1,), (0,)), ((), ()))):
    return lax.dot_general(left, right, dims, preferred_element_type=jnp.float32)


def half(value):
    return value.astype(jnp.bfloat16)


def whole_call(body, out_shape, scratch=()):
    return pl.pallas_call(
        body,
        out_shape=out_shape,
        scratch_shapes=scratch,
        compiler_params=pltpu.CompilerParams(vmem_limit_bytes=VMEM_BYTES),
    )


def ssd_kernel(
    few,
    act_ref,
    gate_ref,
    d_normed_ref,
    run_ref,
    run_t_ref,
    step_t_ref,
    skip_ref,
    norm_gain_ref,
    normed_ref,
    d_gate_ref,
    d_act_ref,
    row_ref,
    col_ref,
    skip_part_ref,
    norm_part_ref,
    decay_ref,
    ssd_ref,
    d_ssd_ref,
):
    count = act_ref.shape[0]
    inner_w = gate_ref.shape[1]
    heads = run_ref.shape[1]
    head_dim = inner_w // heads
    per_tile = LANES // head_dim
    rows = lax.broadcasted_iota(jnp.int32, (count, count), 0)
    cols = lax.broadcasted_iota(jnp.int32, (count, count), 1)
    causal = (lax.rem(rows, few) == lax.rem(cols, few)) & (rows >= cols)
    lane = lax.broadcasted_iota(jnp.int32, (count, LANES), 1)
    low = lane < head_dim
    bc = act_ref[:, inner_w:]
    swapped_float = pltpu.roll(bc.astype(jnp.float32), head_dim, 1)
    swapped = half(swapped_float)
    inner_cb = dot_f32(half(jnp.where(low, swapped_float, 0.0)), bc, contract_cols)
    inner_cb = jnp.where(causal, inner_cb, 0.0)

    for tile in range(inner_w // LANES):
        span = slice(tile * LANES, (tile + 1) * LANES)
        u = act_ref[:, span]
        result = u.astype(jnp.float32) * skip_ref[:, span]
        for place in range(per_tile):
            h = tile * per_tile + place
            spread = run_t_ref[h : h + 1, :] - run_ref[:, h : h + 1]
            decay = jnp.exp(jnp.where(causal, spread, 0.0))
            decay_ref[h] = decay
            weights = half(inner_cb * decay * step_t_ref[h : h + 1, :])
            mine = lane // head_dim == place
            result = result + jnp.where(mine, dot_f32(weights, u), 0.0)
        ssd_ref[:, span] = half(result)

    squares = jnp.zeros((count, LANES), jnp.float32)
    crossed = jnp.zeros((count, LANES), jnp.float32)
    for tile in range(inner_w // LANES):
        span = slice(tile * LANES, (tile + 1) * LANES)
        gate = gate_ref[:, span].astype(jnp.float32)
        gated = ssd_ref[:, span].astype(jnp.float32) * (gate * jax.nn.sigmoid(gate))
        squares = squares + gated * gated
        crossed = crossed + gated * (d_normed_ref[:, span] * norm_gain_ref[:, span])
    mean_square = jnp.sum(squares, axis=1, keepdims=True) / inner_w
    scale_row = lax.rsqrt(mean_square + norm_eps)
    pulled = jnp.sum(crossed, axis=1, keepdims=True) / inner_w * scale_row * scale_row
    for tile in range(inner_w // LANES):
        span = slice(tile * LANES, (tile + 1) * LANES)
        gate = gate_ref[:, span].astype(jnp.float32)
        squashed = jax.nn.sigmoid(gate)
        silu = gate * squashed
        ssd = ssd_ref[:, span].astype(jnp.float32)
        gated = ssd * silu
        scaled = gated * scale_row
        d_normed = d_normed_ref[:, span]
        normed_ref[:, span] = half(scaled * norm_gain_ref[:, span])
        norm_part_ref[:, span] = jnp.sum(d_normed * scaled, axis=0, keepdims=True)
        d_gated = scale_row * (d_normed * norm_gain_ref[:, span] - gated * pulled)
        d_ssd_ref[:, span] = half(d_gated * silu)
        d_gate_ref[:, span] = half(d_gated * ssd * (squashed * (1.0 + gate * (1.0 - squashed))))

    d_cb = jnp.zeros((count, count), jnp.float32)
    for tile in range(inner_w // LANES):
        span = slice(tile * LANES, (tile + 1) * LANES)
        u = act_ref[:, span]
        d_y = d_ssd_ref[:, span]
        d_y_float = d_y.astype(jnp.float32)
        d_u = d_y_float * skip_ref[:, span]
        skip_part_ref[:, span] = jnp.sum(d_y_float * u.astype(jnp.float32), axis=0, keepdims=True)
        for place in range(per_tile):
            h = tile * per_tile + place
            mine = lane // head_dim == place
            d_weights = dot_f32(half(jnp.where(mine, d_y_float, 0.0)), u, contract_cols)
            decay = decay_ref[h]
            step_row = step_t_ref[h : h + 1, :]
            d_scaled = d_weights * decay
            d_cb = d_cb + d_scaled * step_row
            product = d_scaled * inner_cb
            col_ref[h : h + 1, :] = jnp.sum(product, axis=0, keepdims=True)
            row_ref[:, h : h + 1] = jnp.sum(product * step_row, axis=1, keepdims=True)
            weights = half(inner_cb * decay * step_row)
            d_u = d_u + jnp.where(mine, dot_f32(weights, d_y, contract_rows), 0.0)
        d_act_ref[:, span] = half(d_u)
    d_cb = half(jnp.where(causal, d_cb, 0.0))
    d_act_ref[:, inner_w:] = half(
        jnp.where(low, dot_f32(d_cb, swapped, contract_rows), dot_f32(d_cb, swapped))
    )


def sideways(flat, cols):
    rows = flat.shape[0]
    col = lax.rem(lax.broadcasted_iota(jnp.int32, flat.shape, 0), cols)
    left = jnp.where(col > 0, pltpu.roll(flat, 1, 0), 0.0)
    right = jnp.where(col < cols - 1, pltpu.roll(flat, rows - 1, 0), 0.0)
    return left, flat, right


def tall_tile(low_ref, mid_ref, high_ref, span):
    stacked = jnp.concatenate(
        [ref[:, :, :, span].astype(jnp.float32) for ref in (low_ref, mid_ref, high_ref)], axis=1
    )
    return stacked, stacked.reshape(-1, stacked.shape[-1])


def conv_kernel_body(low_ref, mid_ref, high_ref, kernel_ref, bias_ref, before_ref, act_ref):
    row_count, cols = mid_ref.shape[1], mid_ref.shape[2]
    for tile in range(mid_ref.shape[3] // LANES):
        span = slice(tile * LANES, (tile + 1) * LANES)
        stacked, flat = tall_tile(low_ref, mid_ref, high_ref, span)
        total = bias_ref[:, span].reshape(1, 1, 1, -1)
        for col_off, moved in enumerate(sideways(flat, cols)):
            moved = moved.reshape(stacked.shape)
            for row_off in range(3):
                k = 3 * row_off + col_off
                tap = kernel_ref[k : k + 1, span].reshape(1, 1, 1, -1)
                total = total + tap * moved[:, row_off : row_off + row_count]
        before_ref[:, :, :, span] = total
        act_ref[:, :, :, span] = half(total * jax.nn.sigmoid(total))


def d_before_body(d_act_ref, before_ref, d_before_ref, d_half_ref):
    for tile in range(before_ref.shape[3] // LANES):
        span = slice(tile * LANES, (tile + 1) * LANES)
        before = before_ref[:, :, :, span]
        squashed = jax.nn.sigmoid(before)
        slope = squashed * (1.0 + before * (1.0 - squashed))
        d_before = d_act_ref[:, :, :, span].astype(jnp.float32) * slope
        d_before_ref[:, :, :, span] = d_before
        d_half_ref[:, :, :, span] = half(d_before)


def kernel_grad_body(low_ref, mid_ref, high_ref, d_before_ref, part_ref):
    row_count, cols = mid_ref.shape[1], mid_ref.shape[2]
    for tile in range(mid_ref.shape[3] // LANES):
        span = slice(tile * LANES, (tile + 1) * LANES)
        stacked, flat = tall_tile(low_ref, mid_ref, high_ref, span)
        d_before = d_before_ref[:, :, :, span]
        for col_off, moved in enumerate(sideways(flat, cols)):
            moved = moved.reshape(stacked.shape)
            for row_off in range(3):
                product = d_before * moved[:, row_off : row_off + row_count]
                k = 3 * row_off + col_off
                part_ref[k : k + 1, span] = jnp.sum(
                    product.reshape(-1, LANES), axis=0, keepdims=True
                )
        part_ref[9:10, span] = jnp.sum(d_before.reshape(-1, LANES), axis=0, keepdims=True)


def d_mixed_body(low_ref, mid_ref, high_ref, kernel_ref, d_mixed_ref):
    row_count, cols = mid_ref.shape[1], mid_ref.shape[2]
    for tile in range(mid_ref.shape[3] // LANES):
        span = slice(tile * LANES, (tile + 1) * LANES)
        stacked, flat = tall_tile(low_ref, mid_ref, high_ref, span)
        total = jnp.zeros(mid_ref.shape[:3] + (LANES,), jnp.float32)
        for shift, moved in enumerate(sideways(flat, cols)):
            moved = moved.reshape(stacked.shape)
            for row_off in range(3):
                k = 3 * row_off + 2 - shift
                tap = kernel_ref[k : k + 1, span].reshape(1, 1, 1, -1)
                total = total + tap * moved[:, 2 - row_off : 2 - row_off + row_count]
        d_mixed_ref[:, :, :, span] = half(total)


def edges(block):
    count = lax.axis_size("space")
    forward = [(i, i + 1) for i in range(count - 1)]
    backward = [(i + 1, i) for i in range(count - 1)]
    low = lax.ppermute(block[:, -1:], "space", forward)
    high = lax.ppermute(block[:, :1], "space", backward)
    return low, high


def to_sequences(block):
    parts = lax.axis_size("tm")
    frames, tokens, width = block.shape
    few = tokens // parts
    sent = block.reshape(frames, parts, few, width).transpose(1, 0, 2, 3)
    sent = sent.reshape(parts, frames * few, width)
    got = lax.all_to_all(sent, "tm", split_axis=0, concat_axis=0, tiled=True)
    return got.reshape(parts * frames * few, width)


def to_frames(flat, frames):
    parts = lax.axis_size("tm")
    few = flat.shape[0] // (parts * frames)
    width = flat.shape[1]
    got = lax.all_to_all(
        flat.reshape(parts, frames * few, width), "tm", split_axis=0, concat_axis=0, tiled=True
    )
    got = got.reshape(parts, frames, few, width).transpose(1, 0, 2, 3)
    return got.reshape(frames, parts * few, width)


def swapped_over(block, axis, bit):
    pairs = [(i, i ^ (1 << bit)) for i in range(lax.axis_size(axis))]
    return lax.ppermute(block, axis, pairs)


def halve(block, dim, axis, bit):
    mine = lax.rem(lax.axis_index(axis) // (1 << bit), 2)
    sent = half(lax.dynamic_index_in_dim(block, 1 - mine, dim, keepdims=False))
    kept = lax.dynamic_index_in_dim(block, mine, dim, keepdims=False)
    return kept + swapped_over(sent, axis, bit).astype(jnp.float32)


def bits_of(axis):
    return lax.axis_size(axis).bit_length() - 1


def core_halves(block):
    bits = bits_of("tm") + bits_of("space")
    block = block.reshape((2,) * bits + (block.shape[0] >> bits, block.shape[1]))
    return halve(block, bits - 1, "space", 0)


def tm_step(pair, step):
    last = bits_of("tm") - 1
    return [halve(pair[0], last - step, "tm", step), halve(pair[1], 0, "tm", last - step)]


def chip_rows(pair):
    joined = jnp.concatenate(pair, axis=-1)
    space_bits = bits_of("space")
    for bit in range(1, space_bits):
        joined = halve(joined, space_bits - 1 - bit, "space", bit)
    return joined


def sum_everywhere(block):
    for axis in ("space", "tm"):
        for bit in range(bits_of(axis)):
            block = block + swapped_over(block, axis, bit)
    return block


def on_device(
    activations,
    in_proj,
    step_proj,
    step_bias,
    decay_rates,
    conv_kernel,
    conv_bias,
    skip_gain,
    norm_gain,
    out_proj,
    out_cotangent,
):
    frame_count, row_count, col_count, model_width = activations.shape
    inner_w = out_proj.shape[0]
    head_count = step_proj.shape[1]
    head_dim = inner_w // head_count
    conv_w = in_proj.shape[1] - inner_w
    token_count = row_count * col_count
    few = token_count // lax.axis_size("tm")
    grid = (frame_count, row_count, col_count)

    flat_act = activations.reshape(-1, model_width)
    mixed_in = half(dot_f32(flat_act, in_proj[:, inner_w:])).reshape(grid + (conv_w,))
    low, high = edges(mixed_in)
    both = jnp.concatenate([activations, out_cotangent], axis=-1)
    both_seq = to_sequences(both.reshape(frame_count, token_count, -1))
    flat_kernel = conv_kernel.reshape(9, conv_w)
    before, activated = whole_call(
        conv_kernel_body,
        (
            jax.ShapeDtypeStruct(grid + (conv_w,), jnp.float32),
            jax.ShapeDtypeStruct(grid + (conv_w,), jnp.bfloat16),
        ),
    )(low, mixed_in, high, flat_kernel, conv_bias.reshape(1, -1))
    act_seq = to_sequences(activated.reshape(frame_count, token_count, conv_w))

    x_seq, cot_seq = both_seq[:, :model_width], both_seq[:, model_width:]
    count = x_seq.shape[0]
    gate_z = half(dot_f32(x_seq, in_proj[:, :inner_w]))
    step_raw = dot_f32(x_seq, step_proj) + step_bias
    steps = half(jax.nn.softplus(step_raw)).astype(jnp.float32)
    d_normed = dot_f32(cot_seq, out_proj, contract_cols)
    index = jnp.arange(count)
    earlier = (
        (index[:, None] % few == index[None, :] % few) & (index[:, None] >= index[None, :])
    ).astype(jnp.float32)
    running = jnp.dot(earlier, steps * decay_rates, precision=top_precision)
    f32, bf16 = jnp.float32, jnp.bfloat16
    normed, d_gate, d_act_seq, row_sums, col_sums, skip_part, norm_part = whole_call(
        functools.partial(ssd_kernel, few),
        (
            jax.ShapeDtypeStruct((count, inner_w), bf16),
            jax.ShapeDtypeStruct((count, inner_w), bf16),
            jax.ShapeDtypeStruct((count, conv_w), bf16),
            jax.ShapeDtypeStruct((count, head_count), f32),
            jax.ShapeDtypeStruct((head_count, count), f32),
            jax.ShapeDtypeStruct((1, inner_w), f32),
            jax.ShapeDtypeStruct((1, inner_w), f32),
        ),
        (
            pltpu.VMEM((head_count, count, count), f32),
            pltpu.VMEM((count, inner_w), bf16),
            pltpu.VMEM((count, inner_w), bf16),
        ),
    )(
        act_seq,
        gate_z,
        d_normed,
        running,
        running.T,
        steps.T,
        jnp.repeat(skip_gain, head_dim).reshape(1, -1),
        norm_gain.reshape(1, -1),
    )
    d_act = to_frames(d_act_seq, frame_count).reshape(grid + (conv_w,))
    col_turned = col_sums.T
    d_running = col_turned * steps - row_sums
    d_decay = jnp.dot(earlier.T, d_running, precision=top_precision)
    d_steps = half(col_turned + d_decay * decay_rates).astype(f32)
    rate_part = jnp.sum(d_decay * steps, axis=0)
    gain_part = jnp.sum(skip_part.reshape(head_count, head_dim), axis=1)
    d_raw = d_steps * jax.nn.sigmoid(step_raw)
    bias_part = jnp.sum(d_raw, axis=0)
    d_raw_half = half(d_raw)
    early = [
        core_halves(dot_f32(x_seq, jnp.concatenate([d_gate, d_raw_half], axis=1), contract_rows)),
        core_halves(dot_f32(cot_seq, normed, contract_rows)),
    ]
    d_act, early = lax.optimization_barrier((d_act, early))
    early = tm_step(early, 0)

    d_before, d_half = whole_call(
        d_before_body,
        (
            jax.ShapeDtypeStruct(before.shape, f32),
            jax.ShapeDtypeStruct(before.shape, bf16),
        ),
    )(d_act, before)
    d_low, d_high = edges(d_half)
    conv_parts = whole_call(kernel_grad_body, jax.ShapeDtypeStruct((10, conv_w), f32))(
        low, mixed_in, high, d_before
    )
    d_mixed = whole_call(d_mixed_body, jax.ShapeDtypeStruct(before.shape, bf16))(
        d_low, d_before, d_high, flat_kernel
    ).reshape(-1, conv_w)
    cut = conv_w // (2 * LANES) * LANES
    d_mixed, early = lax.optimization_barrier((d_mixed, early))
    late = core_halves(dot_f32(flat_act, d_mixed, contract_rows))
    for step in range(1, bits_of("tm")):
        early = tm_step(early, step)
    small = jnp.concatenate(
        [conv_parts.reshape(-1), norm_part.reshape(-1), bias_part, rate_part, gain_part]
    )

    late, early, normed, d_gate, d_raw_half, d_mixed = lax.optimization_barrier(
        (late, early, normed, d_gate, d_raw_half, d_mixed)
    )
    early = chip_rows(early)
    late = [late[..., :cut], late[..., cut:]]
    for step in range(bits_of("tm")):
        late = tm_step(late, step)
        if step == 0:
            late, small = lax.optimization_barrier((late, small))
    late = chip_rows(late)
    layer_seq = half(dot_f32(normed, out_proj))
    back = to_frames(jnp.concatenate([d_gate, layer_seq, d_raw_half], axis=1), frame_count)
    back = back.reshape(-1, back.shape[-1])
    d_gate_frames = back[:, :inner_w]
    layer_out = back[:, inner_w : 2 * inner_w].reshape(activations.shape)
    d_raw_frames = back[:, 2 * inner_w :]
    grad_input = half(
        dot_f32(d_gate_frames, in_proj[:, :inner_w], contract_cols)
        + dot_f32(d_mixed, in_proj[:, inner_w:], contract_cols)
        + dot_f32(d_raw_frames, step_proj, contract_cols)
    ).reshape(activations.shape)
    grad_in_proj = jnp.concatenate([early[:, :inner_w], late], axis=1)
    grad_step_proj = early[:, inner_w : inner_w + head_count]
    grad_out_proj_t = early[:, inner_w + head_count :]
    small = sum_everywhere(small)
    taps = 9 * conv_w
    sizes = [taps, conv_w, inner_w, head_count, head_count, head_count]
    pieces, start = [], 0
    for size in sizes:
        pieces.append(small[start : start + size])
        start += size
    return (
        layer_out,
        grad_input,
        grad_in_proj,
        grad_step_proj,
        grad_out_proj_t,
        pieces[0].reshape(3, 3, conv_w),
        pieces[1],
        pieces[3],
        pieces[4],
        pieces[5],
        pieces[2],
    )


def solution(mesh):
    placed = (
        P("tm", "space", None, None),
        P(),
        P(),
        P(),
        P(),
        P(),
        P(),
        P(),
        P(),
        P(),
        P("tm", "space", None, None),
    )
    return jax.shard_map(
        on_device,
        mesh=mesh,
        in_specs=placed,
        out_specs=(
            P("tm", "space", None, None),
            P("tm", "space", None, None),
            P(("tm", "space"), None),
            P(("tm", "space"), None),
            P(("tm", "space"), None),
            P(),
            P(),
            P(),
            P(),
            P(),
            P(),
        ),
        check_vma=False,
    )
```
